32 devices in a mesh: fsdp: 8 (over z, core), tp: 4 (over y, x).
Axes of the slice: x: 2, y: 2, z: 4, core: 2. Of those that a mesh axis runs over, the one named last changes fastest.
Arguments:
- tokens: bfloat16 [1024, 16384], P('fsdp', 'tp'), may hold values from -400 to 400
- norm_gain: bfloat16 [16384], P('tp'), may hold values from 0.5 to 1.5
- key_weight: bfloat16 [16384, 1024], P('fsdp', 'tp'), may hold values from -0.046875 to 0.046875
- value_weight: bfloat16 [16384, 1024], P('fsdp', 'tp'), may hold values from -0.046875 to 0.046875
Outputs:
- keys: bfloat16 [1024, 1024], P('fsdp', 'tp')
- values_out: bfloat16 [1024, 1024], P('fsdp', 'tp')
- hessian: float32 [16384, 16384], P('fsdp', 'tp')
The draws below stay inside these ranges and needn't reach their ends.
All inputs are finite; a program needn't handle non-finite values.
Results may differ from the reference program's by a relative error of at most 0.0051.
Values may be sent and summed in bfloat16 or wider, within the bound.
No kernel may reach another device: no remote copies, remote signals or barrier semaphores. Data moves between devices by JAX's collectives and lax.ppermute only.
A program may use at most 192 MiB of HBM per device.

```python
import math
import jax
import jax.numpy as jnp
from jax import lax

D = 16384
KV = 1024
TOKENS = 1024


def draw_tokens(key, part):
    key = jax.random.fold_in(key, 11)
    first, second, third = jax.random.split(key, 3)
    row_scale = jnp.exp(jax.random.uniform(first, (TOKENS, 1), jnp.float32) * math.log(10.0))
    ramp = jnp.arange(D, dtype=jnp.float32)[None, :] / D
    col_scale = jnp.exp(math.log(3.0) * ramp) * jnp.exp(jax.random.uniform(third, (1, D), jnp.float32, -0.69, 0.69))
    base = jnp.clip(jax.random.normal(second, (TOKENS, D), jnp.float32), -5.0, 5.0)
    return (base * row_scale * col_scale).astype(jnp.bfloat16)


def block_scale(own_key, extent, cuts, smallest, largest):
    def one(position, parts):
        heights = jax.random.uniform(jax.random.fold_in(jax.random.fold_in(own_key, 6), position), (parts,), jnp.float32, smallest / len(cuts), largest / len(cuts))
        return jnp.repeat(jnp.exp(heights), extent[position] // parts).reshape((-1,) + (1,) * (len(extent) - position - 1))

    factor_of = one(*cuts[0])
    for cut in cuts[1:]:
        factor_of = factor_of * one(*cut)
    return factor_of


def centred(key, dims, spread, limit, cuts=(), kind=jnp.bfloat16):
    result = spread * jax.random.normal(key, dims, jnp.float32)
    if cuts:
        result = result * block_scale(key, dims, cuts, -0.22, 0.18)
    return jnp.clip(result, -limit, limit).astype(kind)


def setup_inputs(seed: int = 0) -> dict:
    seeds = jax.random.split(jax.random.key(seed), 5)
    return {
        "tokens": draw_tokens(jax.random.fold_in(seeds[4], 71), 0),
        "norm_gain": jnp.clip(1.0 + 0.1 * jax.random.normal(seeds[1], (D,), jnp.float32), 0.5, 1.5).astype(jnp.bfloat16),
        "key_weight": centred(seeds[2], (D, KV), D ** -0.5, 0.046875, ((0, 8), (1, 4))),
        "value_weight": centred(seeds[3], (D, KV), D ** -0.5, 0.046875, ((0, 8), (1, 4))),
    }


def reference(tokens, norm_gain, key_weight, value_weight):
    widened = tokens.astype(jnp.float32)
    power = lax.optimization_barrier(jnp.mean(widened * widened, axis=1, keepdims=True))
    normed = (widened * norm_gain.astype(jnp.float32)[None, :] * lax.rsqrt(power + 1e-05)).astype(jnp.bfloat16)
    keys = jnp.dot(normed, key_weight, preferred_element_type=jnp.float32).astype(jnp.bfloat16)
    values_out = jnp.dot(normed, value_weight, preferred_element_type=jnp.float32).astype(jnp.bfloat16)
    normed_wide = normed.astype(jnp.float32)
    hessian = jnp.dot(normed_wide.T, normed_wide, precision=lax.Precision.HIGHEST) * (2.0 / TOKENS)
    return (keys, values_out, hessian)
```

```python
import functools

import jax
import jax.numpy as jnp
from jax import lax
from jax.experimental import pallas as pl
from jax.experimental.pallas import tpu as pltpu
from jax.sharding import PartitionSpec as P

epsilon = 1e-05
BOTH = ("fsdp", "tp")

LANES = range(2)
NEAR = [(z * 2 + c, (z ^ 1) * 2 + c) for z in range(4) for c in LANES]
MIDDLE = [(z * 2 + c, (3 - z) * 2 + c) for z in (1, 2) for c in LANES]
OUTWARD = [(2 + c, c) for c in LANES] + [(4 + c, 6 + c) for c in LANES]
CORES = [(f, f ^ 1) for f in range(8)]
HOME_TWO = [(c, 4 + c) for c in LANES] + [(6 + c, 2 + c) for c in LANES]
HOME_TWO_BACK = [(2 + c, 6 + c) for c in LANES] + [(4 + c, c) for c in LANES]
HOME_THREE = [(c, 6 + c) for c in LANES] + [(6 + c, c) for c in LANES]


def plane(start, end, depths=range(4)):
    return [
        ((z * 2 + c) * 4 + (z ^ start), (z * 2 + c) * 4 + (z ^ end))
        for z in depths
        for c in LANES
    ]


def tile_kernel(scale, slots, *refs):
    rows, cols, out = refs[:slots], refs[slots : 2 * slots], refs[2 * slots]
    turned = [row[...].T for row in rows]
    width = out.shape[1]
    step = min(width, 1024)
    for left in range(0, width, step):
        total = None
        for row, col in zip(turned, cols):
            product = jnp.dot(
                row, col[:, left : left + step], preferred_element_type=jnp.float32
            )
            total = product if total is None else total + product
        out[:, left : left + step] = total * scale


def hessian_tile(rows, cols, scale):
    slots = len(rows)
    depth, height = rows[0].shape
    width = cols[0].shape[1]
    block = 256
    flops = 2 * slots * depth * height * width
    return pl.pallas_call(
        functools.partial(tile_kernel, scale, slots),
        grid=(height // block,),
        in_specs=[pl.BlockSpec((depth, block), lambda i: (0, i))] * slots
        + [pl.BlockSpec((depth, width), lambda i: (0, 0), pipeline_mode=pl.Buffered(1))] * slots,
        out_specs=pl.BlockSpec((block, width), lambda i: (i, 0)),
        out_shape=jax.ShapeDtypeStruct((height, width), jnp.float32),
        compiler_params=pltpu.CompilerParams(vmem_limit_bytes=40 << 20),
        cost_estimate=pl.CostEstimate(
            flops=flops, bytes_accessed=4 * height * width, transcendentals=0
        ),
    )(*rows, *cols)


def slice_body(tokens, norm_gain, key_weight, value_weight):
    count, width = tokens.shape
    features = width * lax.axis_size("tp")
    half = width // 2
    total_tokens = count * 8
    f, t = lax.axis_index("fsdp"), lax.axis_index("tp")
    z, core = f // 2, f % 2
    role = z ^ t
    middle = (z == 1) | (z == 2)

    def move(x, pairs, axis="fsdp"):
        return lax.ppermute(x, axis, pairs)

    near = move(tokens, NEAR)
    across = move(tokens, MIDDLE)
    own_twin = move(tokens, CORES)

    widened = tokens.astype(jnp.float32)
    partial_power = jnp.sum(widened * widened, axis=1)
    note = jnp.concatenate([partial_power, norm_gain.astype(jnp.float32)])
    notes = lax.all_gather(note, "tp")
    power = jnp.sum(notes[:, :count], axis=0)
    inverse = lax.all_gather(lax.rsqrt(power / features + epsilon), "fsdp")
    row_gain = lax.dynamic_slice(notes, (z, count + core * half), (1, half))
    col_gain = norm_gain.astype(jnp.float32)[None, :]

    outer = move(across, OUTWARD)
    beyond = move(near, MIDDLE)
    last = move(beyond, OUTWARD)
    second = jnp.where(middle, across, outer)
    third = jnp.where(middle, beyond, last)

    def my_half(block):
        return lax.dynamic_slice(block, (0, core * half), (count, half))

    def pick(at_root, at_x, at_y, at_far):
        return jnp.where(
            role == 0, at_root, jnp.where(role == 1, at_x, jnp.where(role == 2, at_y, at_far))
        )

    def spread(block, twin, direct):
        mine, other = my_half(block), my_half(twin)
        mine_x = move(mine, plane(0, 1), BOTH)
        other_y = move(other, plane(0, 2), BOTH)
        mine_far = move(mine_x, plane(1, 3), BOTH)
        other_far = move(other_y, plane(2, 3), BOTH)
        if direct:
            mine_y = move(mine, plane(0, 2), BOTH)
            other_x = move(other, plane(0, 1), BOTH)
        else:
            mine_y = move(mine_far, plane(3, 2), BOTH)
            other_x = move(other_far, plane(3, 1), BOTH)
        return pick(mine, mine_x, mine_y, mine_far), pick(other, other_x, other_y, other_far)

    def norm(block, gain, group):
        scale = lax.dynamic_slice(inverse, (group, 0), (1, count))[0]
        return (block.astype(jnp.float32) * gain * scale[:, None]).astype(jnp.bfloat16)

    sources = (
        (tokens, own_twin, z, False),
        (near, move(near, CORES), z ^ 1, False),
        (second, move(second, CORES), jnp.where(z < 2, 2, 1), True),
        (third, move(third, CORES), jnp.where(z < 2, 3, 0), True),
    )
    rows, cols = [], []
    for block, twin, group, direct in sources:
        mine, other = group * 2 + core, group * 2 + 1 - core
        cols.append(
            jnp.concatenate([norm(block, col_gain, mine), norm(twin, col_gain, other)])
        )
        row_block, row_twin = spread(block, twin, direct)
        rows.append(
            jnp.concatenate([norm(row_block, row_gain, mine), norm(row_twin, row_gain, other)])
        )

    weights = jnp.concatenate([key_weight, value_weight], axis=1)
    parts = [jnp.dot(row, weights, preferred_element_type=jnp.float32) for row in rows]
    sums = [part[:count] + move(part[count:], CORES) for part in parts]
    projected = (
        sums[0]
        + move(sums[1], NEAR)
        + move(sums[2], MIDDLE)
        + move(sums[2], HOME_TWO)
        + move(sums[3], HOME_TWO_BACK)
        + move(sums[3], HOME_THREE)
    ).astype(jnp.bfloat16)
    columns = key_weight.shape[1]
    hessian = hessian_tile(rows, cols, 2.0 / total_tokens)
    return projected[:, :columns], projected[:, columns:], hessian


def general_body(tokens, norm_gain, key_weight, value_weight):
    features = tokens.shape[1] * lax.axis_size("tp")
    total_tokens = tokens.shape[0] * lax.axis_size("fsdp")
    widened = tokens.astype(jnp.float32)
    power = lax.psum(jnp.sum(widened * widened, axis=1), "tp")
    inverse = lax.rsqrt(power / features + epsilon)
    normed = (widened * norm_gain.astype(jnp.float32)[None, :] * inverse[:, None]).astype(
        jnp.bfloat16
    )
    cols = lax.all_gather(normed, "fsdp", axis=0, tiled=True)
    full_rows = lax.all_gather(normed, "tp", axis=1, tiled=True)
    rows = lax.all_to_all(full_rows, "fsdp", split_axis=1, concat_axis=0, tiled=True)
    weights = jnp.concatenate([key_weight, value_weight], axis=1)
    part = jnp.dot(rows, weights, preferred_element_type=jnp.float32)
    projected = lax.psum_scatter(part, "fsdp", scatter_dimension=0, tiled=True).astype(jnp.bfloat16)
    columns = key_weight.shape[1]
    hessian = hessian_tile([rows], [cols], 2.0 / total_tokens)
    return projected[:, :columns], projected[:, columns:], hessian


def solution(mesh):
    small = mesh.shape["fsdp"] == 8 and mesh.shape["tp"] == 4
    placed = (P("fsdp", "tp"), P("tp"), P("fsdp", "tp"), P("fsdp", "tp"))
    return jax.shard_map(
        slice_body if small else general_body,
        mesh=mesh,
        in_specs=placed,
        out_specs=(P("fsdp", "tp"), P("fsdp", "tp"), P("fsdp", "tp")),
        check_vma=False,
    )
```

```python
import functools

import jax
import jax.numpy as jnp
from jax import lax
from jax.experimental import pallas as pl
from jax.experimental.pallas import tpu as pltpu
from jax.sharding import PartitionSpec as P

epsilon = 1e-05

def along(chips):
    return [(start * 2 + c, end * 2 + c) for start, end in chips for c in range(2)]


NEAR = along([(z, z ^ 1) for z in range(4)])
FLIPS = {j: along([(z, z ^ j) for z in range(4)]) for j in (1, 2, 3)}
MIDDLE = along([(1, 2), (2, 1)])
OUTWARD = along([(1, 0), (2, 3)])
CORES = [(f, f ^ 1) for f in range(8)]
SIDES = {k: [(t, t ^ k) for t in range(4)] for k in (1, 2, 3)}


def tile_kernel(scale, slots, *refs):
    rows, cols, out = refs[:slots], refs[slots : 2 * slots], refs[2 * slots]
    together = 2 if slots % 2 == 0 else 1
    groups = [slice(i, i + together) for i in range(0, slots, together)]
    turned = [jnp.concatenate([row[...] for row in rows[g]]).T for g in groups]
    width = out.shape[1]
    step = min(width, 1024)
    for left in range(0, width, step):
        total = None
        for row, group in zip(turned, groups):
            col = jnp.concatenate([c[:, left : left + step] for c in cols[group]])
            product = jnp.dot(row, col, preferred_element_type=jnp.float32)
            total = product if total is None else total + product
        out[:, left : left + step] = total * scale


def hessian_tile(rows, cols, scale):
    slots = len(rows)
    depth, height = rows[0].shape
    width = cols[0].shape[1]
    block = 256
    flops = 2 * slots * depth * height * width
    return pl.pallas_call(
        functools.partial(tile_kernel, scale, slots),
        grid=(height // block,),
        in_specs=[pl.BlockSpec((depth, block), lambda i: (0, i))] * slots
        + [pl.BlockSpec((depth, width), lambda i: (0, 0), pipeline_mode=pl.Buffered(1))] * slots,
        out_specs=pl.BlockSpec((block, width), lambda i: (i, 0)),
        out_shape=jax.ShapeDtypeStruct((height, width), jnp.float32),
        compiler_params=pltpu.CompilerParams(vmem_limit_bytes=40 << 20),
        cost_estimate=pl.CostEstimate(
            flops=flops, bytes_accessed=4 * height * width, transcendentals=0
        ),
    )(*rows, *cols)


def pair_kernel(left, right, out):
    width = left.shape[1]
    out[:, :width] = left[...]
    out[:, width:] = right[...]


def side_by_side(left, right):
    depth, width = left.shape
    block = pl.BlockSpec((depth, width), lambda: (0, 0))
    return pl.pallas_call(
        pair_kernel,
        in_specs=[block, block],
        out_specs=pl.BlockSpec((depth, 2 * width), lambda: (0, 0)),
        out_shape=jax.ShapeDtypeStruct((depth, 2 * width), left.dtype),
        compiler_params=pltpu.CompilerParams(vmem_limit_bytes=16 << 20),
        cost_estimate=pl.CostEstimate(flops=0, bytes_accessed=50_000_000, transcendentals=0),
    )(left, right)


def slice_body(tokens, norm_gain, key_weight, value_weight):
    count, width = tokens.shape
    features = width * 4
    half, quarter = width // 2, count // 4
    total_tokens = count * 8
    f, t = lax.axis_index("fsdp"), lax.axis_index("tp")
    z, core = f // 2, f % 2
    role = z ^ t
    middle = (z == 1) | (z == 2)

    def move(x, pairs, axis="fsdp"):
        return lax.ppermute(x, axis, pairs)

    def reorder(x):
        return jnp.concatenate(
            [lax.dynamic_slice_in_dim(x, (t ^ k) * quarter, quarter) for k in range(4)]
        )

    turned = reorder(tokens)
    near = move(turned, NEAR)
    across = move(turned, MIDDLE)

    pieces = [turned[k * quarter : (k + 1) * quarter] for k in range(4)]
    held = [pieces[0]] + [move(pieces[k], SIDES[k], "tp") for k in (1, 2, 3)]

    widened = tokens.astype(jnp.float32)
    note = jnp.concatenate([jnp.sum(widened * widened, axis=1), norm_gain.astype(jnp.float32)])
    notes = lax.all_gather(note, "tp")
    *held, notes = lax.optimization_barrier((*held, notes))
    power = jnp.sum(notes[:, :count], axis=0)
    scale = lax.rsqrt(power / features + epsilon)
    gains = notes[:, count:]
    col_gain = norm_gain.astype(jnp.float32)[None, :]

    def norm(block, gain, scale):
        return (block.astype(jnp.float32) * gain * scale).astype(jnp.bfloat16)

    rest = lax.dynamic_slice_in_dim(scale, t * quarter, quarter)[:, None]
    quarter_scale, thirds = rest, []
    for _ in range(3):
        part = lax.reduce_precision(rest, 8, 7)
        rest = rest - part
        thirds.append(part.astype(jnp.bfloat16))
    thirds = jnp.concatenate(thirds + [jnp.zeros((quarter, 125), jnp.bfloat16)], axis=1)

    def choose(which):
        piece = jnp.where(
            which == 0,
            held[0],
            jnp.where(which == 1, held[1], jnp.where(which == 2, held[2], held[3])),
        )
        gain = lax.dynamic_slice_in_dim(gains, t ^ which, 1)
        return jnp.concatenate([norm(piece, gain, quarter_scale), thirds], axis=1)

    landed = [choose(role)] + [move(choose(role ^ j), FLIPS[j]) for j in (1, 2, 3)]

    outer = move(across, OUTWARD)
    beyond = move(near, MIDDLE)

    key_weight, value_weight, near, across = lax.optimization_barrier(
        (key_weight, value_weight, near, across)
    )
    weights = side_by_side(key_weight, value_weight)
    *landed, weights = lax.optimization_barrier((*landed, weights))
    landed = jnp.stack(landed)

    def share(which):
        features = lax.dynamic_slice_in_dim(landed, which * half, half, axis=2)
        return jnp.concatenate([features, landed[:, :, width:]], axis=2)

    mine = share(core)
    other = move(share(1 - core), CORES)
    group = jnp.stack([mine, other])
    from_x = move(group, SIDES[1], "tp")
    from_y = move(group, SIDES[2], "tp")
    last = move(beyond, OUTWARD)
    far_mine = move(from_y[0], SIDES[1], "tp")
    far_other = move(from_x[1], SIDES[2], "tp")
    from_x, from_y, turned, near, beyond = lax.optimization_barrier(
        (from_x, from_y, turned, near, beyond)
    )
    quarters = [
        [mine, from_x[0], from_y[0], far_mine],
        [other, from_x[1], from_y[1], far_other],
    ]
    blocks = [turned, near, jnp.where(middle, beyond, outer)]
    twins = [move(block, CORES) for block in blocks]

    def row_part(j, p):
        return jnp.concatenate([g[j, :, :half] for g in quarters[p]])

    sent_scales = [
        [jnp.sum(g[:, :, half:].astype(jnp.float32), axis=2) for g in quarters[p]]
        for p in range(2)
    ]
    scales = [jnp.concatenate(sent_scales[p], axis=1) for p in range(2)]

    def col_parts(j):
        return [norm((blocks, twins)[p][j], col_gain, scales[p][j][:, None]) for p in range(2)]

    rows = [[row_part(j, p) for p in range(2)] for j in range(4)]
    parts = [
        jnp.dot(jnp.concatenate(row), weights, preferred_element_type=jnp.float32) for row in rows
    ]
    own = jnp.stack([part[:count] for part in parts])
    sums = own + move(jnp.stack([part[count:] for part in parts]), CORES)
    homes = [move(sums[j], FLIPS[j]) for j in (1, 2, 3)]

    cols = [col_parts(j) for j in range(3)]
    last, cols = lax.optimization_barrier((last, cols))
    blocks.append(jnp.where(middle, across, last))
    twins.append(move(blocks[3], CORES))
    cols.append(col_parts(3))
    hessian = hessian_tile(sum(rows, []), sum(cols, []), 2.0 / total_tokens)

    hessian, homes = lax.optimization_barrier((hessian, homes))
    projected = sums[0] + homes[0] + homes[1] + homes[2]
    projected = reorder(projected.astype(jnp.bfloat16))
    columns = key_weight.shape[1]
    return projected[:, :columns], projected[:, columns:], hessian


def general_body(tokens, norm_gain, key_weight, value_weight):
    features = tokens.shape[1] * lax.axis_size("tp")
    total_tokens = tokens.shape[0] * lax.axis_size("fsdp")
    widened = tokens.astype(jnp.float32)
    power = lax.psum(jnp.sum(widened * widened, axis=1), "tp")
    inverse = lax.rsqrt(power / features + epsilon)
    normed = (widened * norm_gain.astype(jnp.float32)[None, :] * inverse[:, None]).astype(
        jnp.bfloat16
    )
    cols = lax.all_gather(normed, "fsdp", axis=0, tiled=True)
    full_rows = lax.all_gather(normed, "tp", axis=1, tiled=True)
    rows = lax.all_to_all(full_rows, "fsdp", split_axis=1, concat_axis=0, tiled=True)
    weights = jnp.concatenate([key_weight, value_weight], axis=1)
    part = jnp.dot(rows, weights, preferred_element_type=jnp.float32)
    projected = lax.psum_scatter(part, "fsdp", scatter_dimension=0, tiled=True).astype(jnp.bfloat16)
    columns = key_weight.shape[1]
    hessian = hessian_tile([rows], [cols], 2.0 / total_tokens)
    return projected[:, :columns], projected[:, columns:], hessian


def solution(mesh):
    small = mesh.shape["fsdp"] == 8 and mesh.shape["tp"] == 4
    placed = (P("fsdp", "tp"), P("tp"), P("fsdp", "tp"), P("fsdp", "tp"))
    return jax.shard_map(
        slice_body if small else general_body,
        mesh=mesh,
        in_specs=placed,
        out_specs=(P("fsdp", "tp"), P("fsdp", "tp"), P("fsdp", "tp")),
        check_vma=False,
    )
```

```python
import functools

import jax
import jax.numpy as jnp
from jax import lax
from jax.experimental import pallas as pl
from jax.experimental.pallas import tpu as pltpu
from jax.sharding import PartitionSpec as P

epsilon = 1e-05

def along(chips):
    return [(start * 2 + c, end * 2 + c) for start, end in chips for c in range(2)]


NEAR = along([(z, z ^ 1) for z in range(4)])
FLIPS = {j: along([(z, z ^ j) for z in range(4)]) for j in (1, 2, 3)}
MIDDLE = along([(1, 2), (2, 1)])
OUTWARD = along([(1, 0), (2, 3)])
CORES = [(f, f ^ 1) for f in range(8)]
SIDES = {k: [(t, t ^ k) for t in range(4)] for k in (1, 2, 3)}


def tile_kernel(scale, quarters, *refs):
    rows, cols, out = refs[:quarters], refs[quarters:-1], refs[-1]
    slots = rows[0].shape[0]
    each = len(cols) // slots
    turned = [jnp.concatenate([row[j] for row in rows]).T for j in range(slots)]
    width = out.shape[1]
    step = min(width, 1024)
    for left in range(0, width, step):
        total = None
        for j, row in enumerate(turned):
            group = cols[each * j : each * (j + 1)]
            col = jnp.concatenate([c[:, left : left + step] for c in group])
            product = jnp.dot(row, col, preferred_element_type=jnp.float32)
            total = product if total is None else total + product
        out[:, left : left + step] = total * scale


def hessian_tile(rows, cols, scale):
    _, slots, depth, height = rows[0][0].shape
    col_depth, width = cols[0].shape
    block = 256
    return pl.pallas_call(
        functools.partial(tile_kernel, scale, len(rows)),
        grid=(height // block,),
        in_specs=[
            pl.BlockSpec((None, slots, depth, block), lambda i, p=p: (p, 0, 0, i)) for _, p in rows
        ]
        + [pl.BlockSpec((col_depth, width), lambda i: (0, 0), pipeline_mode=pl.Buffered(1))]
        * len(cols),
        out_specs=pl.BlockSpec((block, width), lambda i: (i, 0)),
        out_shape=jax.ShapeDtypeStruct((height, width), jnp.float32),
        compiler_params=pltpu.CompilerParams(vmem_limit_bytes=40 << 20),
        cost_estimate=pl.CostEstimate(
            flops=2 * len(cols) * col_depth * height * width,
            bytes_accessed=4 * height * width,
            transcendentals=0,
        ),
    )(*(array for array, _ in rows), *cols)


def pair_kernel(left, right, out):
    width = left.shape[1]
    out[:, :width] = left[...]
    out[:, width:] = right[...]


def side_by_side(left, right):
    depth, width = left.shape
    block = pl.BlockSpec((depth, width), lambda: (0, 0))
    return pl.pallas_call(
        pair_kernel,
        in_specs=[block, block],
        out_specs=pl.BlockSpec((depth, 2 * width), lambda: (0, 0)),
        out_shape=jax.ShapeDtypeStruct((depth, 2 * width), left.dtype),
        compiler_params=pltpu.CompilerParams(vmem_limit_bytes=16 << 20),
        cost_estimate=pl.CostEstimate(flops=0, bytes_accessed=50_000_000, transcendentals=0),
    )(left, right)


def slice_body(tokens, norm_gain, key_weight, value_weight):
    count, width = tokens.shape
    features = width * 4
    half, quarter = width // 2, count // 4
    total_tokens = count * 8
    f, t = lax.axis_index("fsdp"), lax.axis_index("tp")
    z, core = f // 2, f % 2
    role = z ^ t
    middle = (z == 1) | (z == 2)

    def move(x, pairs, axis="fsdp"):
        return lax.ppermute(x, axis, pairs)

    def reorder(x):
        return jnp.concatenate(
            [lax.dynamic_slice_in_dim(x, (t ^ k) * quarter, quarter) for k in range(4)]
        )

    turned = reorder(tokens)
    near = move(turned, NEAR)
    across = move(turned, MIDDLE)

    pieces = [turned[k * quarter : (k + 1) * quarter] for k in range(4)]
    held = [pieces[0]] + [move(pieces[k], SIDES[k], "tp") for k in (1, 2, 3)]

    widened = tokens.astype(jnp.float32)
    note = jnp.concatenate([jnp.sum(widened * widened, axis=1), norm_gain.astype(jnp.float32)])
    notes = lax.all_gather(note, "tp")
    *held, notes = lax.optimization_barrier((*held, notes))
    power = jnp.sum(notes[:, :count], axis=0)
    scale = lax.rsqrt(power / features + epsilon)
    gains = notes[:, count:]
    col_gain = norm_gain.astype(jnp.float32)[None, :]

    def norm(block, gain, scale):
        return (block.astype(jnp.float32) * gain * scale).astype(jnp.bfloat16)

    quarter_scale = lax.dynamic_slice_in_dim(scale, t * quarter, quarter)[:, None]
    rest = reorder(scale).reshape(4, quarter).T
    thirds = []
    for _ in range(3):
        part = lax.reduce_precision(rest, 8, 7)
        rest = rest - part
        thirds.append(part.astype(jnp.bfloat16))
    thirds = jnp.concatenate(thirds + [jnp.zeros((quarter, 116), jnp.bfloat16)], axis=1)

    def choose(which):
        piece = jnp.where(
            which == 0,
            held[0],
            jnp.where(which == 1, held[1], jnp.where(which == 2, held[2], held[3])),
        )
        gain = lax.dynamic_slice_in_dim(gains, t ^ which, 1)
        return jnp.concatenate([norm(piece, gain, quarter_scale), thirds], axis=1)

    landed = [choose(role)] + [move(choose(role ^ j), FLIPS[j]) for j in (1, 2, 3)]

    outer = move(across, OUTWARD)
    beyond = move(near, MIDDLE)

    key_weight, value_weight, near, across = lax.optimization_barrier(
        (key_weight, value_weight, near, across)
    )
    weights = side_by_side(key_weight, value_weight)
    *landed, weights = lax.optimization_barrier((*landed, weights))
    def share(which):
        return jnp.stack(
            [lax.dynamic_slice_in_dim(block, which * half, half, axis=1) for block in landed]
        )

    group = jnp.stack([share(core), move(share(1 - core), CORES)])
    from_x = move(group, SIDES[1], "tp")
    from_y = move(group, SIDES[2], "tp")
    last = move(beyond, OUTWARD)
    from_x, from_y, turned, near, beyond = lax.optimization_barrier(
        (from_x, from_y, turned, near, beyond)
    )
    far = [move(from_y[0], SIDES[1], "tp"), move(from_x[1], SIDES[2], "tp")]
    sent = jnp.stack([block[:, width:].astype(jnp.float32) for block in landed])
    lane = lax.broadcasted_iota(jnp.int32, sent.shape, 2)
    own_scales = jnp.concatenate(
        [jnp.sum(jnp.where((lane % 4 == k) & (lane < 12), sent, 0.0), axis=2) for k in range(4)],
        axis=1,
    )
    scales = [own_scales, move(own_scales, CORES)]
    blocks = [turned, near, jnp.where(middle, beyond, outer)]
    twins = [move(block, CORES) for block in blocks]

    def col_parts(j):
        return [norm((blocks, twins)[p][j], col_gain, scales[p][j][:, None]) for p in range(2)]

    def project(block):
        flat = block.reshape(-1, half)
        product = jnp.dot(flat, weights, preferred_element_type=jnp.float32)
        return product.reshape(*block.shape[:-1], -1)

    parts = [project(block) for block in (group, from_x, from_y)]
    parts = [
        jnp.stack([part[p] for part in parts] + [project(far[p])], axis=1).reshape(4, count, -1)
        for p in range(2)
    ]
    sums = parts[0] + move(parts[1], CORES)
    homes = [move(sums[j], FLIPS[j]) for j in (1, 2, 3)]

    cols = [col_parts(j) for j in range(3)]
    last, cols = lax.optimization_barrier((last, cols))
    blocks.append(jnp.where(middle, across, last))
    twins.append(move(blocks[3], CORES))
    cols.append(col_parts(3))
    rows = [(block, p) for p in range(2) for block in (group, from_x, from_y, far[p][None])]
    rows = [(block, min(p, block.shape[0] - 1)) for block, p in rows]
    hessian = hessian_tile(rows, sum(cols, []), 2.0 / total_tokens)

    hessian, homes = lax.optimization_barrier((hessian, homes))
    projected = sums[0] + homes[0] + homes[1] + homes[2]
    projected = reorder(projected.astype(jnp.bfloat16))
    columns = key_weight.shape[1]
    return projected[:, :columns], projected[:, columns:], hessian


def general_body(tokens, norm_gain, key_weight, value_weight):
    features = tokens.shape[1] * lax.axis_size("tp")
    total_tokens = tokens.shape[0] * lax.axis_size("fsdp")
    widened = tokens.astype(jnp.float32)
    power = lax.psum(jnp.sum(widened * widened, axis=1), "tp")
    inverse = lax.rsqrt(power / features + epsilon)
    normed = (widened * norm_gain.astype(jnp.float32)[None, :] * inverse[:, None]).astype(
        jnp.bfloat16
    )
    cols = lax.all_gather(normed, "fsdp", axis=0, tiled=True)
    full_rows = lax.all_gather(normed, "tp", axis=1, tiled=True)
    rows = lax.all_to_all(full_rows, "fsdp", split_axis=1, concat_axis=0, tiled=True)
    weights = jnp.concatenate([key_weight, value_weight], axis=1)
    part = jnp.dot(rows, weights, preferred_element_type=jnp.float32)
    projected = lax.psum_scatter(part, "fsdp", scatter_dimension=0, tiled=True).astype(jnp.bfloat16)
    columns = key_weight.shape[1]
    hessian = hessian_tile([(rows[None, None], 0)], [cols], 2.0 / total_tokens)
    return projected[:, :columns], projected[:, columns:], hessian


def solution(mesh):
    small = mesh.shape["fsdp"] == 8 and mesh.shape["tp"] == 4
    placed = (P("fsdp", "tp"), P("tp"), P("fsdp", "tp"), P("fsdp", "tp"))
    return jax.shard_map(
        slice_body if small else general_body,
        mesh=mesh,
        in_specs=placed,
        out_specs=(P("fsdp", "tp"), P("fsdp", "tp"), P("fsdp", "tp")),
        check_vma=False,
    )
```

```python
import functools

import jax
import jax.numpy as jnp
from jax import lax
from jax.experimental import pallas as pl
from jax.experimental.pallas import tpu as pltpu
from jax.sharding import PartitionSpec as P

epsilon = 1e-05

def along(chips):
    return [(start * 2 + c, end * 2 + c) for start, end in chips for c in range(2)]


NEAR = along([(z, z ^ 1) for z in range(4)])
FLIPS = {j: along([(z, z ^ j) for z in range(4)]) for j in (1, 2, 3)}
MIDDLE = along([(1, 2), (2, 1)])
OUTWARD = along([(1, 0), (2, 3)])
CORES = [(f, f ^ 1) for f in range(8)]
SIDES = {k: [(t, t ^ k) for t in range(4)] for k in (1, 2, 3)}


def tile_kernel(scale, quarters, *refs):
    rows, cols, out = refs[:quarters], refs[quarters:-1], refs[-1]
    slots = rows[0].shape[0]
    each = len(cols) // slots
    turned = [jnp.concatenate([row[j] for row in rows]).T for j in range(slots)]
    width = out.shape[1]
    step = min(width, 1024)
    for left in range(0, width, step):
        total = None
        for j, row in enumerate(turned):
            group = cols[each * j : each * (j + 1)]
            col = jnp.concatenate([c[:, left : left + step] for c in group])
            product = jnp.dot(row, col, preferred_element_type=jnp.float32)
            total = product if total is None else total + product
        out[:, left : left + step] = total * scale


def hessian_tile(rows, cols, scale):
    _, slots, depth, height = rows[0][0].shape
    col_depth, width = cols[0].shape
    block = 256
    return pl.pallas_call(
        functools.partial(tile_kernel, scale, len(rows)),
        grid=(height // block,),
        in_specs=[
            pl.BlockSpec((None, slots, depth, block), lambda i, p=p: (p, 0, 0, i)) for _, p in rows
        ]
        + [pl.BlockSpec((col_depth, width), lambda i: (0, 0), pipeline_mode=pl.Buffered(1))]
        * len(cols),
        out_specs=pl.BlockSpec((block, width), lambda i: (i, 0)),
        out_shape=jax.ShapeDtypeStruct((height, width), jnp.float32),
        compiler_params=pltpu.CompilerParams(vmem_limit_bytes=40 << 20),
        cost_estimate=pl.CostEstimate(
            flops=2 * len(cols) * col_depth * height * width,
            bytes_accessed=4 * height * width,
            transcendentals=0,
        ),
    )(*(array for array, _ in rows), *cols)


def pair_kernel(left, right, out):
    width = left.shape[1]
    out[:, :width] = left[...]
    out[:, width:] = right[...]


def side_by_side(left, right):
    depth, width = left.shape
    block = pl.BlockSpec((depth, width), lambda: (0, 0))
    return pl.pallas_call(
        pair_kernel,
        in_specs=[block, block],
        out_specs=pl.BlockSpec((depth, 2 * width), lambda: (0, 0)),
        out_shape=jax.ShapeDtypeStruct((depth, 2 * width), left.dtype),
        compiler_params=pltpu.CompilerParams(vmem_limit_bytes=16 << 20),
        cost_estimate=pl.CostEstimate(flops=0, bytes_accessed=50_000_000, transcendentals=0),
    )(left, right)


def pieces_kernel(places, *refs):
    held, (notes, scale, thirds) = refs[:4], refs[4:7]
    outs, kept = refs[7:11], refs[11]
    role, t = places[0], places[1]
    width = held[0].shape[1]
    first = notes.shape[1] - width
    for k in range(4):
        gain = notes[pl.ds(t ^ k, 1), :][:, first:]
        kept[k] = (held[k][...].astype(jnp.float32) * gain * scale[...]).astype(kept.dtype)
    for j in range(4):
        outs[j][:, :width] = kept[role ^ j]
        outs[j][:, width:] = thirds[...]


def row_pieces(places, held, notes, scale, thirds):
    quarter, width = held[0].shape

    def whole(*shape):
        return pl.BlockSpec(shape, lambda: (0,) * len(shape))

    out = whole(quarter, width + thirds.shape[1])
    shape = jax.ShapeDtypeStruct((quarter, width + thirds.shape[1]), thirds.dtype)
    return list(
        pl.pallas_call(
            pieces_kernel,
            in_specs=[pl.BlockSpec(memory_space=pltpu.SMEM)]
            + [whole(quarter, width)] * 4
            + [whole(*notes.shape), whole(*scale.shape), whole(*thirds.shape)],
            out_specs=[out] * 4,
            out_shape=[shape] * 4,
            scratch_shapes=[pltpu.VMEM((4, quarter, width), thirds.dtype)],
            compiler_params=pltpu.CompilerParams(vmem_limit_bytes=16 << 20),
            cost_estimate=pl.CostEstimate(
                flops=0, bytes_accessed=16 * quarter * width, transcendentals=0
            ),
        )(places, *held, notes, scale, thirds)
    )


def slice_body(tokens, norm_gain, key_weight, value_weight):
    count, width = tokens.shape
    features = width * 4
    half, quarter = width // 2, count // 4
    total_tokens = count * 8
    f, t = lax.axis_index("fsdp"), lax.axis_index("tp")
    z, core = f // 2, f % 2
    role = z ^ t
    middle = (z == 1) | (z == 2)

    def move(x, pairs, axis="fsdp"):
        return lax.ppermute(x, axis, pairs)

    def reorder(x):
        return jnp.concatenate(
            [lax.dynamic_slice_in_dim(x, (t ^ k) * quarter, quarter) for k in range(4)]
        )

    turned = reorder(tokens)
    near = move(tokens, NEAR)
    across = move(tokens, MIDDLE)

    pieces = [turned[k * quarter : (k + 1) * quarter] for k in range(4)]
    held = [pieces[0]] + [move(pieces[k], SIDES[k], "tp") for k in (1, 2, 3)]

    widened = tokens.astype(jnp.float32)
    note = jnp.concatenate([jnp.sum(widened * widened, axis=1), norm_gain.astype(jnp.float32)])
    notes = lax.all_gather(note, "tp")
    *held, notes = lax.optimization_barrier((*held, notes))
    power = jnp.sum(notes[:, :count], axis=0)
    scale = lax.rsqrt(power / features + epsilon)
    col_gain = norm_gain.astype(jnp.float32)[None, :]

    def norm(block, gain, scale):
        return (block.astype(jnp.float32) * gain * scale).astype(jnp.bfloat16)

    quarter_scale = lax.dynamic_slice_in_dim(scale, t * quarter, quarter)[:, None]
    rest = reorder(scale).reshape(4, quarter).T
    thirds = []
    for _ in range(3):
        part = lax.reduce_precision(rest, 8, 7)
        rest = rest - part
        thirds.append(part.astype(jnp.bfloat16))
    thirds = jnp.concatenate(thirds + [jnp.zeros((quarter, 116), jnp.bfloat16)], axis=1)

    leaving = row_pieces(jnp.stack([role, t]), held, notes, quarter_scale, thirds)
    landed = leaving[:1] + [move(leaving[j], FLIPS[j]) for j in (1, 2, 3)]

    outer = move(across, OUTWARD)
    beyond = move(near, MIDDLE)

    key_weight, value_weight, near, across = lax.optimization_barrier(
        (key_weight, value_weight, near, across)
    )
    weights = side_by_side(key_weight, value_weight)
    *landed, weights = lax.optimization_barrier((*landed, weights))
    def share(which):
        return jnp.stack(
            [lax.dynamic_slice_in_dim(block, which * half, half, axis=1) for block in landed]
        )

    group = jnp.stack([share(core), move(share(1 - core), CORES)])
    from_x = move(group, SIDES[1], "tp")
    from_y = move(group, SIDES[2], "tp")
    last = move(beyond, OUTWARD)
    from_x, from_y, tokens, near, beyond = lax.optimization_barrier(
        (from_x, from_y, tokens, near, beyond)
    )
    far = [move(from_y[0], SIDES[1], "tp"), move(from_x[1], SIDES[2], "tp")]
    sent = jnp.stack([block[:, width:].astype(jnp.float32) for block in landed])
    lane = lax.broadcasted_iota(jnp.int32, sent.shape, 2)
    own_scales = jnp.concatenate(
        [jnp.sum(jnp.where((lane % 4 == k) & (lane < 12), sent, 0.0), axis=2) for k in range(4)],
        axis=1,
    )
    scales = [own_scales, move(own_scales, CORES)]
    blocks = [tokens, near, jnp.where(middle, beyond, outer)]
    twins = [move(block, CORES) for block in blocks]

    def col_parts(j):
        return [
            norm(reorder((blocks, twins)[p][j]), col_gain, scales[p][j][:, None]) for p in range(2)
        ]

    def project(block):
        flat = block.reshape(-1, half)
        product = jnp.dot(flat, weights, preferred_element_type=jnp.float32)
        return product.reshape(*block.shape[:-1], -1)

    parts = [project(block) for block in (group, from_x, from_y)]
    parts = [
        jnp.stack([part[p] for part in parts] + [project(far[p])], axis=1).reshape(4, count, -1)
        for p in range(2)
    ]
    sums = parts[0] + move(parts[1], CORES)
    homes = [move(sums[j], FLIPS[j]) for j in (1, 2, 3)]

    cols = [col_parts(j) for j in range(3)]
    last, cols = lax.optimization_barrier((last, cols))
    blocks.append(jnp.where(middle, across, last))
    twins.append(move(blocks[3], CORES))
    cols.append(col_parts(3))
    rows = [(block, p) for p in range(2) for block in (group, from_x, from_y, far[p][None])]
    rows = [(block, min(p, block.shape[0] - 1)) for block, p in rows]
    hessian = hessian_tile(rows, sum(cols, []), 2.0 / total_tokens)

    hessian, homes = lax.optimization_barrier((hessian, homes))
    projected = sums[0] + homes[0] + homes[1] + homes[2]
    projected = reorder(projected.astype(jnp.bfloat16))
    columns = key_weight.shape[1]
    return projected[:, :columns], projected[:, columns:], hessian


def general_body(tokens, norm_gain, key_weight, value_weight):
    features = tokens.shape[1] * lax.axis_size("tp")
    total_tokens = tokens.shape[0] * lax.axis_size("fsdp")
    widened = tokens.astype(jnp.float32)
    power = lax.psum(jnp.sum(widened * widened, axis=1), "tp")
    inverse = lax.rsqrt(power / features + epsilon)
    normed = (widened * norm_gain.astype(jnp.float32)[None, :] * inverse[:, None]).astype(
        jnp.bfloat16
    )
    cols = lax.all_gather(normed, "fsdp", axis=0, tiled=True)
    full_rows = lax.all_gather(normed, "tp", axis=1, tiled=True)
    rows = lax.all_to_all(full_rows, "fsdp", split_axis=1, concat_axis=0, tiled=True)
    weights = jnp.concatenate([key_weight, value_weight], axis=1)
    part = jnp.dot(rows, weights, preferred_element_type=jnp.float32)
    projected = lax.psum_scatter(part, "fsdp", scatter_dimension=0, tiled=True).astype(jnp.bfloat16)
    columns = key_weight.shape[1]
    hessian = hessian_tile([(rows[None, None], 0)], [cols], 2.0 / total_tokens)
    return projected[:, :columns], projected[:, columns:], hessian


def solution(mesh):
    small = mesh.shape["fsdp"] == 8 and mesh.shape["tp"] == 4
    placed = (P("fsdp", "tp"), P("tp"), P("fsdp", "tp"), P("fsdp", "tp"))
    return jax.shard_map(
        slice_body if small else general_body,
        mesh=mesh,
        in_specs=placed,
        out_specs=(P("fsdp", "tp"), P("fsdp", "tp"), P("fsdp", "tp")),
        check_vma=False,
    )
```

```python
import functools

import jax
import jax.numpy as jnp
from jax import lax
from jax.experimental import pallas as pl
from jax.experimental.pallas import tpu as pltpu
from jax.sharding import PartitionSpec as P

epsilon = 1e-05

def along(chips):
    return [(start * 2 + c, end * 2 + c) for start, end in chips for c in range(2)]


NEAR = along([(z, z ^ 1) for z in range(4)])
FLIPS = {j: along([(z, z ^ j) for z in range(4)]) for j in (1, 2, 3)}
MIDDLE = along([(1, 2), (2, 1)])
OUTWARD = along([(1, 0), (2, 3)])
CORES = [(f, f ^ 1) for f in range(8)]
SIDES = {k: [(t, t ^ k) for t in range(4)] for k in (1, 2, 3)}


def tile_kernel(scale, quarters, *refs):
    rows, cols, out = refs[:quarters], refs[quarters:-1], refs[-1]
    slots = rows[0].shape[0]
    each = len(cols) // slots
    turned = [jnp.concatenate([row[j] for row in rows]).T for j in range(slots)]
    width = out.shape[1]
    step = min(width, 1024)
    for left in range(0, width, step):
        total = None
        for j, row in enumerate(turned):
            group = cols[each * j : each * (j + 1)]
            col = jnp.concatenate([c[:, left : left + step] for c in group])
            product = jnp.dot(row, col, preferred_element_type=jnp.float32)
            total = product if total is None else total + product
        out[:, left : left + step] = total * scale


def hessian_tile(rows, cols, scale):
    _, slots, depth, height = rows[0][0].shape
    col_depth, width = cols[0].shape
    block = 256
    return pl.pallas_call(
        functools.partial(tile_kernel, scale, len(rows)),
        grid=(height // block,),
        in_specs=[
            pl.BlockSpec((None, slots, depth, block), lambda i, p=p: (p, 0, 0, i)) for _, p in rows
        ]
        + [pl.BlockSpec((col_depth, width), lambda i: (0, 0), pipeline_mode=pl.Buffered(1))]
        * len(cols),
        out_specs=pl.BlockSpec((block, width), lambda i: (i, 0)),
        out_shape=jax.ShapeDtypeStruct((height, width), jnp.float32),
        compiler_params=pltpu.CompilerParams(vmem_limit_bytes=40 << 20),
        cost_estimate=pl.CostEstimate(
            flops=2 * len(cols) * col_depth * height * width,
            bytes_accessed=4 * height * width,
            transcendentals=0,
        ),
    )(*(array for array, _ in rows), *cols)


def pair_kernel(left, right, out):
    width = left.shape[1]
    out[:, :width] = left[...]
    out[:, width:] = right[...]


def side_by_side(left, right):
    depth, width = left.shape
    block = pl.BlockSpec((depth, width), lambda: (0, 0))
    return pl.pallas_call(
        pair_kernel,
        in_specs=[block, block],
        out_specs=pl.BlockSpec((depth, 2 * width), lambda: (0, 0)),
        out_shape=jax.ShapeDtypeStruct((depth, 2 * width), left.dtype),
        compiler_params=pltpu.CompilerParams(vmem_limit_bytes=16 << 20),
        cost_estimate=pl.CostEstimate(flops=0, bytes_accessed=50_000_000, transcendentals=0),
    )(left, right)


def pieces_kernel(places, *refs):
    held, (notes, scale, thirds) = refs[:4], refs[4:7]
    outs, kept = refs[7:11], refs[11]
    role, t = places[0], places[1]
    width = held[0].shape[1]
    first = notes.shape[1] - width
    for k in range(4):
        gain = notes[pl.ds(t ^ k, 1), :][:, first:]
        kept[k] = (held[k][...].astype(jnp.float32) * gain * scale[...]).astype(kept.dtype)
    for j in range(4):
        outs[j][:, :width] = kept[role ^ j]
        outs[j][:, width:] = thirds[...]


def row_pieces(places, held, notes, scale, thirds):
    quarter, width = held[0].shape

    def whole(*shape):
        return pl.BlockSpec(shape, lambda: (0,) * len(shape))

    out = whole(quarter, width + thirds.shape[1])
    shape = jax.ShapeDtypeStruct((quarter, width + thirds.shape[1]), thirds.dtype)
    return list(
        pl.pallas_call(
            pieces_kernel,
            in_specs=[pl.BlockSpec(memory_space=pltpu.SMEM)]
            + [whole(quarter, width)] * 4
            + [whole(*notes.shape), whole(*scale.shape), whole(*thirds.shape)],
            out_specs=[out] * 4,
            out_shape=[shape] * 4,
            scratch_shapes=[pltpu.VMEM((4, quarter, width), thirds.dtype)],
            compiler_params=pltpu.CompilerParams(vmem_limit_bytes=16 << 20),
            cost_estimate=pl.CostEstimate(
                flops=0, bytes_accessed=16 * quarter * width, transcendentals=0
            ),
        )(places, *held, notes, scale, thirds)
    )


def slice_body(tokens, norm_gain, key_weight, value_weight):
    count, width = tokens.shape
    features = width * 4
    half, quarter = width // 2, count // 4
    total_tokens = count * 8
    f, t = lax.axis_index("fsdp"), lax.axis_index("tp")
    z, core = f // 2, f % 2
    role = z ^ t
    middle = (z == 1) | (z == 2)

    def move(x, pairs, axis="fsdp"):
        return lax.ppermute(x, axis, pairs)

    def reorder(x):
        return jnp.concatenate(
            [lax.dynamic_slice_in_dim(x, (t ^ k) * quarter, quarter) for k in range(4)]
        )

    turned = reorder(tokens)
    near = move(tokens, NEAR)
    across = move(tokens, MIDDLE)

    pieces = [turned[k * quarter : (k + 1) * quarter] for k in range(4)]
    held = [pieces[0]] + [move(pieces[k], SIDES[k], "tp") for k in (1, 2, 3)]

    widened = tokens.astype(jnp.float32)
    note = jnp.concatenate([jnp.sum(widened * widened, axis=1), norm_gain.astype(jnp.float32)])
    notes = lax.all_gather(note, "tp")
    *held, notes = lax.optimization_barrier((*held, notes))
    power = jnp.sum(notes[:, :count], axis=0)
    scale = lax.rsqrt(power / features + epsilon)
    col_gain = norm_gain.astype(jnp.float32)[None, :]

    def norm(block, gain, scale):
        return (block.astype(jnp.float32) * gain * scale).astype(jnp.bfloat16)

    quarter_scale = lax.dynamic_slice_in_dim(scale, t * quarter, quarter)[:, None]
    rest = reorder(scale).reshape(4, quarter).T
    thirds = []
    for _ in range(3):
        part = lax.reduce_precision(rest, 8, 7)
        rest = rest - part
        thirds.append(part.astype(jnp.bfloat16))
    thirds = jnp.concatenate(thirds + [jnp.zeros((quarter, 116), jnp.bfloat16)], axis=1)

    leaving = row_pieces(jnp.stack([role, t]), held, notes, quarter_scale, thirds)
    landed = leaving[:1] + [move(leaving[j], FLIPS[j]) for j in (1, 2, 3)]

    outer = move(across, OUTWARD)
    beyond = move(near, MIDDLE)

    key_weight, value_weight, near, across = lax.optimization_barrier(
        (key_weight, value_weight, near, across)
    )
    weights = side_by_side(key_weight, value_weight)
    *landed, weights = lax.optimization_barrier((*landed, weights))
    def share(which):
        return jnp.stack(
            [lax.dynamic_slice_in_dim(block, which * half, half, axis=1) for block in landed]
        )

    group = jnp.stack([share(core), move(share(1 - core), CORES)])
    from_x = move(group, SIDES[1], "tp")
    from_y = move(group, SIDES[2], "tp")
    last = move(beyond, OUTWARD)
    sent = jnp.stack([block[:, width:].astype(jnp.float32) for block in landed])
    lane = lax.broadcasted_iota(jnp.int32, sent.shape, 2)
    own_scales = jnp.concatenate(
        [jnp.sum(jnp.where((lane % 4 == k) & (lane < 12), sent, 0.0), axis=2) for k in range(4)],
        axis=1,
    )
    scales = [own_scales, move(own_scales, CORES)]
    blocks = [tokens, near]
    twins = [move(block, CORES) for block in blocks]

    def col_parts(j):
        return [
            norm(reorder((blocks, twins)[p][j]), col_gain, scales[p][j][:, None]) for p in range(2)
        ]

    cols = [col_parts(j) for j in range(2)]
    from_x, from_y, beyond, cols = lax.optimization_barrier((from_x, from_y, beyond, cols))
    far = [move(from_y[0], SIDES[1], "tp"), move(from_x[1], SIDES[2], "tp")]
    blocks.append(jnp.where(middle, beyond, outer))
    twins.append(move(blocks[2], CORES))
    cols.append(col_parts(2))

    def project(block):
        flat = block.reshape(-1, half)
        product = jnp.dot(flat, weights, preferred_element_type=jnp.float32)
        return product.reshape(*block.shape[:-1], -1)

    parts = [project(block) for block in (group, from_x, from_y)]
    parts = [
        jnp.stack([part[p] for part in parts] + [project(far[p])], axis=1).reshape(4, count, -1)
        for p in range(2)
    ]
    sums = parts[0] + move(parts[1], CORES)
    homes = [move(sums[j], FLIPS[j]) for j in (1, 2, 3)]

    last, cols = lax.optimization_barrier((last, cols))
    blocks.append(jnp.where(middle, across, last))
    twins.append(move(blocks[3], CORES))
    cols.append(col_parts(3))
    rows = [(block, p) for p in range(2) for block in (group, from_x, from_y, far[p][None])]
    rows = [(block, min(p, block.shape[0] - 1)) for block, p in rows]
    hessian = hessian_tile(rows, sum(cols, []), 2.0 / total_tokens)

    hessian, homes = lax.optimization_barrier((hessian, homes))
    projected = sums[0] + homes[0] + homes[1] + homes[2]
    projected = reorder(projected.astype(jnp.bfloat16))
    columns = key_weight.shape[1]
    return projected[:, :columns], projected[:, columns:], hessian


def general_body(tokens, norm_gain, key_weight, value_weight):
    features = tokens.shape[1] * lax.axis_size("tp")
    total_tokens = tokens.shape[0] * lax.axis_size("fsdp")
    widened = tokens.astype(jnp.float32)
    power = lax.psum(jnp.sum(widened * widened, axis=1), "tp")
    inverse = lax.rsqrt(power / features + epsilon)
    normed = (widened * norm_gain.astype(jnp.float32)[None, :] * inverse[:, None]).astype(
        jnp.bfloat16
    )
    cols = lax.all_gather(normed, "fsdp", axis=0, tiled=True)
    full_rows = lax.all_gather(normed, "tp", axis=1, tiled=True)
    rows = lax.all_to_all(full_rows, "fsdp", split_axis=1, concat_axis=0, tiled=True)
    weights = jnp.concatenate([key_weight, value_weight], axis=1)
    part = jnp.dot(rows, weights, preferred_element_type=jnp.float32)
    projected = lax.psum_scatter(part, "fsdp", scatter_dimension=0, tiled=True).astype(jnp.bfloat16)
    columns = key_weight.shape[1]
    hessian = hessian_tile([(rows[None, None], 0)], [cols], 2.0 / total_tokens)
    return projected[:, :columns], projected[:, columns:], hessian


def solution(mesh):
    small = mesh.shape["fsdp"] == 8 and mesh.shape["tp"] == 4
    placed = (P("fsdp", "tp"), P("tp"), P("fsdp", "tp"), P("fsdp", "tp"))
    return jax.shard_map(
        slice_body if small else general_body,
        mesh=mesh,
        in_specs=placed,
        out_specs=(P("fsdp", "tp"), P("fsdp", "tp"), P("fsdp", "tp")),
        check_vma=False,
    )
```

```python
import functools

import jax
import jax.numpy as jnp
from jax import lax
from jax.experimental import pallas as pl
from jax.experimental.pallas import tpu as pltpu
from jax.sharding import PartitionSpec as P

epsilon = 1e-05

def along(chips):
    return [(start * 2 + c, end * 2 + c) for start, end in chips for c in range(2)]


NEAR = along([(z, z ^ 1) for z in range(4)])
FLIPS = {j: along([(z, z ^ j) for z in range(4)]) for j in (1, 2, 3)}
MIDDLE = along([(1, 2), (2, 1)])
OUTWARD = along([(1, 0), (2, 3)])
CORES = [(f, f ^ 1) for f in range(8)]
SIDES = {k: [(t, t ^ k) for t in range(4)] for k in (1, 2, 3)}


def tile_kernel(scale, quarters, *refs):
    rows, cols, out = refs[:quarters], refs[quarters:-1], refs[-1]
    slots = rows[0].shape[0]
    each = len(cols) // slots
    turned = [jnp.concatenate([row[j] for row in rows]).T for j in range(slots)]
    width = out.shape[1]
    step = min(width, 1024)
    for left in range(0, width, step):
        total = None
        for j, row in enumerate(turned):
            group = cols[each * j : each * (j + 1)]
            col = jnp.concatenate([c[:, left : left + step] for c in group])
            product = jnp.dot(row, col, preferred_element_type=jnp.float32)
            total = product if total is None else total + product
        out[:, left : left + step] = total * scale


def hessian_tile(rows, cols, scale):
    _, slots, depth, height = rows[0][0].shape
    col_depth, width = cols[0].shape
    block = 256
    return pl.pallas_call(
        functools.partial(tile_kernel, scale, len(rows)),
        grid=(height // block,),
        in_specs=[
            pl.BlockSpec((None, slots, depth, block), lambda i, p=p: (p, 0, 0, i)) for _, p in rows
        ]
        + [pl.BlockSpec((col_depth, width), lambda i: (0, 0), pipeline_mode=pl.Buffered(1))]
        * len(cols),
        out_specs=pl.BlockSpec((block, width), lambda i: (i, 0)),
        out_shape=jax.ShapeDtypeStruct((height, width), jnp.float32),
        compiler_params=pltpu.CompilerParams(vmem_limit_bytes=40 << 20),
        cost_estimate=pl.CostEstimate(
            flops=2 * len(cols) * col_depth * height * width,
            bytes_accessed=4 * height * width,
            transcendentals=0,
        ),
    )(*(array for array, _ in rows), *cols)


def pair_kernel(left, right, out):
    width = left.shape[1]
    out[:, :width] = left[...]
    out[:, width:] = right[...]


def side_by_side(left, right):
    depth, width = left.shape
    block = pl.BlockSpec((depth, width), lambda: (0, 0))
    return pl.pallas_call(
        pair_kernel,
        in_specs=[block, block],
        out_specs=pl.BlockSpec((depth, 2 * width), lambda: (0, 0)),
        out_shape=jax.ShapeDtypeStruct((depth, 2 * width), left.dtype),
        compiler_params=pltpu.CompilerParams(vmem_limit_bytes=16 << 20),
        cost_estimate=pl.CostEstimate(flops=0, bytes_accessed=50_000_000, transcendentals=0),
    )(left, right)


def pieces_kernel(places, *refs):
    held, (notes, scale, thirds) = refs[:4], refs[4:7]
    outs, kept = refs[7:11], refs[11]
    role, t = places[0], places[1]
    width = held[0].shape[1]
    first = notes.shape[1] - width
    for k in range(4):
        gain = notes[pl.ds(t ^ k, 1), :][:, first:]
        kept[k] = (held[k][...].astype(jnp.float32) * gain * scale[...]).astype(kept.dtype)
    for j in range(4):
        outs[j][:, :width] = kept[role ^ j]
        outs[j][:, width:] = thirds[...]


def row_pieces(places, held, notes, scale, thirds):
    quarter, width = held[0].shape

    def whole(*shape):
        return pl.BlockSpec(shape, lambda: (0,) * len(shape))

    out = whole(quarter, width + thirds.shape[1])
    shape = jax.ShapeDtypeStruct((quarter, width + thirds.shape[1]), thirds.dtype)
    return list(
        pl.pallas_call(
            pieces_kernel,
            in_specs=[pl.BlockSpec(memory_space=pltpu.SMEM)]
            + [whole(quarter, width)] * 4
            + [whole(*notes.shape), whole(*scale.shape), whole(*thirds.shape)],
            out_specs=[out] * 4,
            out_shape=[shape] * 4,
            scratch_shapes=[pltpu.VMEM((4, quarter, width), thirds.dtype)],
            compiler_params=pltpu.CompilerParams(vmem_limit_bytes=16 << 20),
            cost_estimate=pl.CostEstimate(
                flops=0, bytes_accessed=16 * quarter * width, transcendentals=0
            ),
        )(places, *held, notes, scale, thirds)
    )


def halves_kernel(core, *refs):
    blocks, mine, leaving = refs[:4], refs[4], refs[5]
    half = mine.shape[2]
    kept = pl.multiple_of(core[0] * half, 128)
    given = pl.multiple_of((1 - core[0]) * half, 128)
    for j, block in enumerate(blocks):
        mine[j] = block[:, pl.ds(kept, half)]
        leaving[j] = block[:, pl.ds(given, half)]


def halves_apart(core, blocks, half):
    block = pl.BlockSpec(blocks[0].shape, lambda: (0, 0))
    shape = (len(blocks), blocks[0].shape[0], half)
    out = pl.BlockSpec(shape, lambda: (0, 0, 0))
    return pl.pallas_call(
        halves_kernel,
        in_specs=[pl.BlockSpec(memory_space=pltpu.SMEM)] + [block] * len(blocks),
        out_specs=[out] * 2,
        out_shape=[jax.ShapeDtypeStruct(shape, blocks[0].dtype)] * 2,
        compiler_params=pltpu.CompilerParams(vmem_limit_bytes=16 << 20),
        cost_estimate=pl.CostEstimate(flops=0, bytes_accessed=2_000_000, transcendentals=0),
    )(core, *blocks)


def slice_body(tokens, norm_gain, key_weight, value_weight):
    count, width = tokens.shape
    features = width * 4
    half, quarter = width // 2, count // 4
    total_tokens = count * 8
    f, t = lax.axis_index("fsdp"), lax.axis_index("tp")
    z, core = f // 2, f % 2
    role = z ^ t
    middle = (z == 1) | (z == 2)

    def move(x, pairs, axis="fsdp"):
        return lax.ppermute(x, axis, pairs)

    def reorder(x):
        return jnp.concatenate(
            [lax.dynamic_slice_in_dim(x, (t ^ k) * quarter, quarter) for k in range(4)]
        )

    turned = reorder(tokens)
    near = move(tokens, NEAR)
    across = move(tokens, MIDDLE)

    pieces = [turned[k * quarter : (k + 1) * quarter] for k in range(4)]
    held = [pieces[0]] + [move(pieces[k], SIDES[k], "tp") for k in (1, 2, 3)]

    widened = tokens.astype(jnp.float32)
    note = jnp.concatenate([jnp.sum(widened * widened, axis=1), norm_gain.astype(jnp.float32)])
    notes = lax.all_gather(note, "tp")
    *held, notes = lax.optimization_barrier((*held, notes))
    power = jnp.sum(notes[:, :count], axis=0)
    scale = lax.rsqrt(power / features + epsilon)
    col_gain = norm_gain.astype(jnp.float32)[None, :]

    def norm(block, gain, scale):
        return (block.astype(jnp.float32) * gain * scale).astype(jnp.bfloat16)

    quarter_scale = lax.dynamic_slice_in_dim(scale, t * quarter, quarter)[:, None]
    rest = reorder(scale).reshape(4, quarter).T
    thirds = []
    for _ in range(3):
        part = lax.reduce_precision(rest, 8, 7)
        rest = rest - part
        thirds.append(part.astype(jnp.bfloat16))
    thirds = jnp.concatenate(thirds + [jnp.zeros((quarter, 116), jnp.bfloat16)], axis=1)

    leaving = row_pieces(jnp.stack([role, t]), held, notes, quarter_scale, thirds)
    landed = leaving[:1] + [move(leaving[j], FLIPS[j]) for j in (1, 2, 3)]

    outer = move(across, OUTWARD)
    beyond = move(near, MIDDLE)

    key_weight, value_weight, near, across = lax.optimization_barrier(
        (key_weight, value_weight, near, across)
    )
    weights = side_by_side(key_weight, value_weight)
    *landed, weights = lax.optimization_barrier((*landed, weights))
    mine, leaving = halves_apart(core[None], landed, half)
    group = jnp.stack([mine, move(leaving, CORES)])
    from_x = move(group, SIDES[1], "tp")
    from_y = move(group, SIDES[2], "tp")
    last = move(beyond, OUTWARD)
    sent = jnp.stack([block[:, width:].astype(jnp.float32) for block in landed])
    lane = lax.broadcasted_iota(jnp.int32, sent.shape, 2)
    own_scales = jnp.concatenate(
        [jnp.sum(jnp.where((lane % 4 == k) & (lane < 12), sent, 0.0), axis=2) for k in range(4)],
        axis=1,
    )
    scales = [own_scales, move(own_scales, CORES)]
    blocks = [tokens, near]
    twins = [move(block, CORES) for block in blocks]

    def col_parts(j):
        return [
            norm(reorder((blocks, twins)[p][j]), col_gain, scales[p][j][:, None]) for p in range(2)
        ]

    cols = [col_parts(j) for j in range(2)]
    from_x, from_y, beyond, cols = lax.optimization_barrier((from_x, from_y, beyond, cols))
    far = [move(from_y[0], SIDES[1], "tp"), move(from_x[1], SIDES[2], "tp")]
    blocks.append(jnp.where(middle, beyond, outer))
    twins.append(move(blocks[2], CORES))
    cols.append(col_parts(2))

    def project(block):
        flat = block.reshape(-1, half)
        product = jnp.dot(flat, weights, preferred_element_type=jnp.float32)
        return product.reshape(*block.shape[:-1], -1)

    parts = [project(block) for block in (group, from_x, from_y)]
    parts = [
        jnp.stack([part[p] for part in parts] + [project(far[p])], axis=1).reshape(4, count, -1)
        for p in range(2)
    ]
    sums = parts[0] + move(parts[1], CORES)
    homes = [move(sums[j], FLIPS[j]) for j in (1, 2, 3)]

    last, cols = lax.optimization_barrier((last, cols))
    blocks.append(jnp.where(middle, across, last))
    twins.append(move(blocks[3], CORES))
    cols.append(col_parts(3))
    rows = [(block, p) for p in range(2) for block in (group, from_x, from_y, far[p][None])]
    rows = [(block, min(p, block.shape[0] - 1)) for block, p in rows]
    hessian = hessian_tile(rows, sum(cols, []), 2.0 / total_tokens)

    hessian, homes = lax.optimization_barrier((hessian, homes))
    projected = sums[0] + homes[0] + homes[1] + homes[2]
    projected = reorder(projected.astype(jnp.bfloat16))
    columns = key_weight.shape[1]
    return projected[:, :columns], projected[:, columns:], hessian


def general_body(tokens, norm_gain, key_weight, value_weight):
    features = tokens.shape[1] * lax.axis_size("tp")
    total_tokens = tokens.shape[0] * lax.axis_size("fsdp")
    widened = tokens.astype(jnp.float32)
    power = lax.psum(jnp.sum(widened * widened, axis=1), "tp")
    inverse = lax.rsqrt(power / features + epsilon)
    normed = (widened * norm_gain.astype(jnp.float32)[None, :] * inverse[:, None]).astype(
        jnp.bfloat16
    )
    cols = lax.all_gather(normed, "fsdp", axis=0, tiled=True)
    full_rows = lax.all_gather(normed, "tp", axis=1, tiled=True)
    rows = lax.all_to_all(full_rows, "fsdp", split_axis=1, concat_axis=0, tiled=True)
    weights = jnp.concatenate([key_weight, value_weight], axis=1)
    part = jnp.dot(rows, weights, preferred_element_type=jnp.float32)
    projected = lax.psum_scatter(part, "fsdp", scatter_dimension=0, tiled=True).astype(jnp.bfloat16)
    columns = key_weight.shape[1]
    hessian = hessian_tile([(rows[None, None], 0)], [cols], 2.0 / total_tokens)
    return projected[:, :columns], projected[:, columns:], hessian


def solution(mesh):
    small = mesh.shape["fsdp"] == 8 and mesh.shape["tp"] == 4
    placed = (P("fsdp", "tp"), P("tp"), P("fsdp", "tp"), P("fsdp", "tp"))
    return jax.shard_map(
        slice_body if small else general_body,
        mesh=mesh,
        in_specs=placed,
        out_specs=(P("fsdp", "tp"), P("fsdp", "tp"), P("fsdp", "tp")),
        check_vma=False,
    )
```
